32 devices in a mesh: grp: 2 (over y), tm: 16 (over z, x, core).
Axes of the slice: x: 2, y: 2, z: 4, core: 2. Of those that a mesh axis runs over, the one named last changes fastest.
Arguments:
- initial_weights: float32 [512], replicated, may hold values from 0.1 to 1
- leave_rate: float32 [512], replicated, may hold values from 0.001 to 0.5
- block_weights: float32 [4, 2, 128, 128], replicated, may hold values from 0.1 to 1
- block_cols: int32 [4, 2], replicated, may hold values from 0 to 3, as said below
- emission_weights: float32 [4, 512], replicated, may hold values from 0.02 to 1
- symbols: int32 [768], P(('grp', 'tm')), parts along dimension 0, may hold values from 0 to 3
Outputs:
- occupancy: float32 [768, 512], P(('grp', 'tm')), parts along dimension 0
- log_norm: float32 [768], P(('grp', 'tm')), parts along dimension 0
The draws below stay inside these ranges and needn't reach their ends.
There are 2 independent parts, one for each index of `grp`. The reference program is written for one: setup_inputs(seed, part) draws one part's arguments, and reference() takes and returns one part's arrays. A program takes and returns all parts, laid end to end along the dimension named above; an argument that names none is the same for every part. Nothing has to cross between parts.
Inputs may be any that keep to these rules, and one draw needn't show every extreme that they name: Row r of block_cols holds 2 different block columns, the first of them r.
All inputs are finite; a program needn't handle non-finite values.
Results may differ from the reference program's by a relative error of at most 0.0003.
Values sent between devices are 32-bit elements; how exact they have to be, the bound alone decides.
A program may use at most 64 MiB of HBM per device.

```python
import math
import jax
import jax.numpy as jnp
from jax import lax

S = 512
BLOCK = 128
NBLK = 4
KB = 2
V = 4
T_SIZE = 384


def draw_block_cols(key, part):
    row_numbers = jnp.arange(NBLK, dtype=jnp.int32)
    row_keys = jax.random.split(key, NBLK)
    offsets = jax.vmap(lambda row_key: jax.random.permutation(row_key, NBLK - 1))(row_keys)[:, :KB - 1] + 1
    others = (row_numbers[:, None] + offsets.astype(jnp.int32)) % NBLK
    return jnp.concatenate([row_numbers[:, None], others], axis=1).astype(jnp.int32)


def set_ends(array, rng, low, high):
    dims = array.shape
    index_at = [jax.random.randint(jax.random.fold_in(rng, axis), (), 0, dims[axis]) for axis in range(len(dims))]
    array = array.at[tuple(index_at)].set(low)
    longest = dims.index(max(dims))
    index_at[longest] = (index_at[longest] + 1) % dims[longest]
    return array.at[tuple(index_at)].set(high)


def setup_inputs(seed: int = 0, part: int = 0) -> dict:
    key_of = jax.random.split(jax.random.key(seed), 7)
    part_splits = jax.random.split(jax.random.fold_in(key_of[6], part), 7)
    return {
        "initial_weights": jnp.clip(jnp.exp(jax.random.uniform(key_of[0], (S,), jnp.float32, math.log(0.1), math.log(1.0))), 0.1, 1.0),
        "leave_rate": jnp.clip(jnp.exp(jax.random.uniform(key_of[1], (S,), jnp.float32, math.log(0.001), math.log(0.5))), 0.001, 0.5),
        "block_weights": jnp.clip(jnp.exp(jax.random.uniform(key_of[2], (NBLK, KB, BLOCK, BLOCK), jnp.float32, math.log(0.1), math.log(1.0))), 0.1, 1.0),
        "block_cols": draw_block_cols(jax.random.fold_in(key_of[6], 71), part),
        "emission_weights": jnp.clip(jnp.exp(jax.random.uniform(key_of[4], (V, S), jnp.float32, math.log(0.02), math.log(1.0))), 0.02, 1.0),
        "symbols": set_ends(jax.random.randint(part_splits[5], (T_SIZE,), 0, V), jax.random.fold_in(part_splits[5], 1), 0, V - 1).astype(jnp.int32),
    }


exact_mode = lax.Precision.HIGHEST


def reference(initial_weights, leave_rate, block_weights, block_cols, emission_weights, symbols):
    states = NBLK * BLOCK
    placement = (block_cols[:, :, None] == jnp.arange(NBLK, dtype=jnp.int32)[None, None, :]).astype(jnp.float32)
    dense_weights = jnp.einsum('rkc,rkij->ricj', placement, block_weights, precision=exact_mode).reshape(states, states)
    spread_rows = dense_weights / jnp.sum(dense_weights, axis=1, keepdims=True)
    transition = jnp.diag(1.0 - leave_rate) + leave_rate[:, None] * spread_rows
    emission = emission_weights / jnp.sum(emission_weights, axis=0, keepdims=True)
    emission_rows = jnp.take(emission, symbols, axis=0)
    start_vector = initial_weights / jnp.sum(initial_weights)

    def forward_step(previous, row_probs):
        unscaled = jnp.dot(previous, transition, precision=exact_mode) * row_probs
        normalizer = jnp.sum(unscaled)
        scaled = unscaled / normalizer
        return scaled, (scaled, jnp.log(normalizer))

    final_forward, (forward_vectors, log_norm) = lax.scan(forward_step, start_vector, emission_rows)

    def backward_step(following, row_probs):
        unscaled = jnp.dot(transition, row_probs * following, precision=exact_mode)
        scaled = unscaled / jnp.sum(unscaled)
        return scaled, scaled

    last_vector = jnp.full((states,), 1.0 / states, jnp.float32)
    final_backward, earlier_vectors = lax.scan(backward_step, last_vector, emission_rows[1:], reverse=True)
    backward_vectors = jnp.concatenate([earlier_vectors, last_vector[None, :]], axis=0)
    joint_terms = forward_vectors * backward_vectors
    occupancy = states * joint_terms / jnp.sum(joint_terms, axis=1, keepdims=True)
    return occupancy, log_norm
```

```python
import functools
import jax
import jax.numpy as jnp
from jax import lax
from jax.experimental import pallas as pl
from jax.experimental.pallas import tpu as pltpu
from jax.sharding import PartitionSpec as P

f32 = jnp.float32
bf16 = jnp.bfloat16
SUBS = 4
NN = (((1,), (0,)), ((), ()))
NT = (((1,), (1,)), ((), ()))


def split(x):
    hi = x.astype(bf16)
    return hi, (x - hi.astype(f32)).astype(bf16)


def dot(a, b, dims=NN):
    return lax.dot_general(a, b, dims, preferred_element_type=f32)


def thin(x, hi, lo, dims=NN):
    top = x.astype(bf16).astype(f32)
    both = jnp.concatenate([top, x - top], axis=0).astype(bf16)
    first = dot(both, hi, dims)
    second = dot(both, lo, dims)
    return first[:8] + (first[8:] + second[:8])


def kernel(init_ref, leave_ref, bw_ref, cols_ref, em_ref, sym_ref, occ_ref, ln_ref,
           w_ref, w_hi, w_lo, x_ref, p_hi, p_lo, q_hi, q_lo, e_ref, u_ref, b_ref,
           f_in, f_out, b_in, b_out, f_send, f_recv, b_send, b_recv):
    pos = lax.axis_index("tm")
    count = lax.axis_size("tm")
    nblk, kb, block, _ = bw_ref.shape
    states = nblk * block
    symbols = em_ref.shape[0]
    steps = occ_ref.shape[0]
    per = steps // SUBS

    barrier = pltpu.get_barrier_semaphore()

    @pl.when(pos > 0)
    def _():
        pl.semaphore_signal(barrier, inc=1, device_id={"tm": pos - 1})

    @pl.when(pos < count - 1)
    def _():
        pl.semaphore_signal(barrier, inc=1, device_id={"tm": pos + 1})

    leave = leave_ref[...]
    stay = 1.0 - leave
    leave_col = jnp.transpose(jnp.broadcast_to(leave, (128, states)))
    for r in range(nblk):
        total = jnp.sum(bw_ref[r, 0], axis=1, keepdims=True)
        for k in range(1, kb):
            total = total + jnp.sum(bw_ref[r, k], axis=1, keepdims=True)
        scale = leave_col[r * block:(r + 1) * block, :] / total
        for c in range(nblk):
            acc = bw_ref[r, 0] * jnp.where(cols_ref[r, 0] == c, 1.0, 0.0)
            for k in range(1, kb):
                acc = acc + bw_ref[r, k] * jnp.where(cols_ref[r, k] == c, 1.0, 0.0)
            acc = acc * scale
            hi, lo = split(acc)
            rs = slice(r * block, (r + 1) * block)
            cs = slice(c * block, (c + 1) * block)
            w_ref[rs, cs] = acc
            w_hi[rs, cs] = hi
            w_lo[rs, cs] = lo

    em = em_ref[...]
    em = em / jnp.sum(em, axis=0, keepdims=True)
    e_ref[...] = jnp.zeros_like(e_ref)
    for j in range(per):
        for g in range(SUBS):
            s = sym_ref[g * per + j]
            row = jnp.zeros((1, states), f32)
            for v in range(symbols):
                row = row + em[v:v + 1] * jnp.where(s == v, 1.0, 0.0)
            e_ref[j, g:g + 1, :] = row

    eye = (lax.broadcasted_iota(jnp.int32, (states, states), 0)
           == lax.broadcasted_iota(jnp.int32, (states, states), 1))
    full_step = jnp.where(eye, jnp.broadcast_to(stay, (states, states)), 0.0) + w_ref[...]
    for g in range(SUBS):
        x_ref[g] = full_step * e_ref[0, g:g + 1, :]

    def advance(j, carry):
        for g in range(SUBS):
            x = x_ref[g]
            xb = x.astype(bf16)
            acc = dot(xb, w_hi[...]) + dot(xb, w_lo[...])
            x_ref[g] = (x * stay + acc) * e_ref[j, g:g + 1, :]
        return carry

    lax.fori_loop(1, per, advance, 0)

    for g in range(SUBS):
        x = x_ref[g]
        x = x * (1.0 / jnp.max(x))
        hi, lo = split(x)
        p_hi[g] = hi
        p_lo[g] = lo

    def joined(a, b):
        return dot(a[0], b[0]) + (dot(a[0], b[1]) + dot(a[1], b[0]))

    left = joined((p_hi[0], p_lo[0]), (p_hi[1], p_lo[1]))
    x_ref[0] = left
    right = joined((p_hi[2], p_lo[2]), (p_hi[3], p_lo[3]))
    x_ref[1] = right
    whole = joined(split(x_ref[0]), split(x_ref[1]))
    hi, lo = split(whole * (1.0 / jnp.max(whole)))
    q_hi[...] = hi
    q_lo[...] = lo

    f_copy = pltpu.make_async_remote_copy(
        src_ref=f_out, dst_ref=f_in, send_sem=f_send, recv_sem=f_recv,
        device_id={"tm": lax.rem(pos + 1, count)})
    b_copy = pltpu.make_async_remote_copy(
        src_ref=b_out, dst_ref=b_in, send_sem=b_send, recv_sem=b_recv,
        device_id={"tm": lax.rem(pos + count - 1, count)})

    inner = jnp.logical_and(pos > 0, pos < count - 1)

    @pl.when(inner)
    def _():
        pl.semaphore_wait(barrier, 2)

    @pl.when(jnp.logical_not(inner))
    def _():
        pl.semaphore_wait(barrier, 1)

    def forward_hop():
        @pl.when(pos == 0)
        def _():
            f_in[...] = init_ref[...]

        @pl.when(pos > 0)
        def _():
            f_copy.wait_recv()

        @pl.when(pos < count - 1)
        def _():
            v = f_in[...]
            out = thin(jnp.broadcast_to(v, (8, states)), q_hi[...], q_lo[...])
            f_out[...] = out[0:1] * (1.0 / jnp.sum(v))
            f_copy.start()

    def backward_hop():
        @pl.when(pos == count - 1)
        def _():
            b_in[...] = jnp.full((1, states), 1.0 / states, f32)

        @pl.when(pos < count - 1)
        def _():
            b_copy.wait_recv()

        @pl.when(pos > 0)
        def _():
            w = b_in[...]
            out = thin(jnp.broadcast_to(w, (8, states)), q_hi[...], q_lo[...], NT)
            b_out[...] = out[0:1] * (1.0 / jnp.sum(w))
            b_copy.start()

    @pl.when(2 * pos < count)
    def _():
        forward_hop()
        backward_hop()

    @pl.when(2 * pos >= count)
    def _():
        backward_hop()
        forward_hop()

    def unit(x):
        return x * (1.0 / jnp.sum(x, axis=1, keepdims=True))

    fs = [unit(f_in[...])]
    for g in range(SUBS - 1):
        nxt = thin(jnp.broadcast_to(fs[-1], (8, states)), p_hi[g], p_lo[g])
        fs.append(unit(nxt[0:1]))
    bs = [unit(b_in[...])]
    for g in range(SUBS - 1, 0, -1):
        nxt = thin(jnp.broadcast_to(bs[-1], (8, states)), p_hi[g], p_lo[g], NT)
        bs.append(unit(nxt[0:1]))
    bs = bs[::-1]
    pad = [jnp.zeros((8 - SUBS, states), f32)]
    f = jnp.concatenate(fs + pad, axis=0)
    b = jnp.concatenate(bs + pad, axis=0)
    b_ref[per - 1] = b
    for i in range(per):
        f = (f * stay + thin(f, w_hi[...], w_lo[...])) * e_ref[i]
        u_ref[i] = f
        j = per - 1 - i
        if j > 0:
            m = b * e_ref[j]
            b = m * stay + thin(m, w_hi[...], w_lo[...], NT)
            b_ref[j - 1] = b

    before = jnp.ones((8, 1), f32)
    for i in range(per):
        u = u_ref[i]
        here = jnp.sum(u, axis=1, keepdims=True)
        logs = jnp.log(here / before)
        before = here
        bb = b_ref[i]
        joint = (u / here) * (bb / jnp.sum(bb, axis=1, keepdims=True))
        occ = states * joint / jnp.sum(joint, axis=1, keepdims=True)
        for g in range(SUBS):
            occ_ref[g * per + i:g * per + i + 1, :] = occ[g:g + 1]
            ln_ref[g * per + i:g * per + i + 1, :] = logs[g:g + 1]

    @pl.when(pos < count - 1)
    def _():
        f_copy.wait_send()

    @pl.when(pos > 0)
    def _():
        b_copy.wait_send()


def body(initial_weights, leave_rate, block_weights, block_cols, emission_weights, symbols):
    states = leave_rate.shape[0]
    steps = symbols.shape[0]
    per = steps // SUBS
    vmem = pl.BlockSpec(memory_space=pltpu.VMEM)
    smem = pl.BlockSpec(memory_space=pltpu.SMEM)
    square = (states, states)
    row = pltpu.VMEM((1, states), f32)
    occupancy, log_norm = pl.pallas_call(
        kernel,
        out_shape=(jax.ShapeDtypeStruct((steps, states), f32),
                   jax.ShapeDtypeStruct((steps, 1), f32)),
        in_specs=[vmem, vmem, vmem, smem, vmem, smem],
        out_specs=(vmem, vmem),
        scratch_shapes=[
            pltpu.VMEM(square, f32), pltpu.VMEM(square, bf16), pltpu.VMEM(square, bf16),
            pltpu.VMEM((SUBS,) + square, f32),
            pltpu.VMEM((SUBS,) + square, bf16), pltpu.VMEM((SUBS,) + square, bf16),
            pltpu.VMEM(square, bf16), pltpu.VMEM(square, bf16),
            pltpu.VMEM((per, 8, states), f32), pltpu.VMEM((per, 8, states), f32),
            pltpu.VMEM((per, 8, states), f32),
            row, row, row, row,
            pltpu.SemaphoreType.DMA, pltpu.SemaphoreType.DMA,
            pltpu.SemaphoreType.DMA, pltpu.SemaphoreType.DMA,
        ],
        compiler_params=pltpu.CompilerParams(
            collective_id=0, has_side_effects=True, vmem_limit_bytes=48 * 1024 * 1024),
    )(initial_weights[None, :], leave_rate[None, :], block_weights, block_cols,
      emission_weights, symbols)
    return occupancy, log_norm[:, 0]


def solution(mesh):
    placed = (P(), P(), P(), P(), P(), P(("grp", "tm")))
    return jax.shard_map(
        body,
        mesh=mesh,
        in_specs=placed,
        out_specs=(P(("grp", "tm"), None), P(("grp", "tm"))),
        check_vma=False,
    )
```

```python
import functools
import jax
import jax.numpy as jnp
from jax import lax
from jax.experimental import pallas as pl
from jax.experimental.pallas import tpu as pltpu
from jax.sharding import PartitionSpec as P

f32 = jnp.float32
bf16 = jnp.bfloat16
SUBS = 4
NN = (((1,), (0,)), ((), ()))
NT = (((1,), (1,)), ((), ()))


def split(x):
    hi = x.astype(bf16)
    return hi, (x - hi.astype(f32)).astype(bf16)


def dot(a, b, dims=NN):
    return lax.dot_general(a, b, dims, preferred_element_type=f32)


def thin(x, hi, lo, dims=NN):
    top = x.astype(bf16).astype(f32)
    both = jnp.concatenate([top, x - top], axis=0).astype(bf16)
    first = dot(both, hi, dims)
    second = dot(both, lo, dims)
    return first[:8] + (first[8:] + second[:8])


def kernel(init_ref, leave_ref, bw_hbm, cols_hbm, em_hbm, sym_hbm, occ_ref, ln_ref,
           bw_ref, cols_ref, em_ref, sym_ref, in_sems,
           w_ref, w_hi, w_lo, x_ref, p_hi, p_lo, h_hi, h_lo, q_hi, q_lo, e_ref, u_ref, b_ref, l_ref,
           mine, got_cols, got_rows, f_in, f_out, b_in, b_out, f_side, b_side, side_out,
           x_send, x_recv, f_send, f_recv, b_send, b_recv, s_send, s_recv):
    pos = lax.axis_index("tm")
    count = lax.axis_size("tm")
    chips = count // 2
    chip = lax.div(pos, 2)
    core = lax.rem(pos, 2)
    partner = chip * 2 + (1 - core)
    below = lax.rem(chip + chips - 1, chips) * 2
    above = lax.rem(chip + 1, chips) * 2
    nblk, kb, block, _ = bw_ref.shape
    states = nblk * block
    symbols = em_ref.shape[0]
    steps = occ_ref.shape[0]
    per = steps // SUBS
    half = states // 2

    loads = [pltpu.make_async_copy(src, dst, in_sems.at[i]) for i, (src, dst) in enumerate(
        [(bw_hbm, bw_ref), (cols_hbm, cols_ref), (em_hbm, em_ref), (sym_hbm, sym_ref)])]
    for load in loads:
        load.start()

    barrier = pltpu.get_barrier_semaphore()

    pl.semaphore_signal(barrier, inc=1, device_id={"tm": partner})

    @pl.when(chip > 0)
    def _():
        for c in range(2):
            pl.semaphore_signal(barrier, inc=1, device_id={"tm": below + c})

    @pl.when(chip < chips - 1)
    def _():
        for c in range(2):
            pl.semaphore_signal(barrier, inc=1, device_id={"tm": above + c})

    leave = leave_ref[...]
    stay = 1.0 - leave
    leave_col = jnp.transpose(jnp.broadcast_to(leave, (128, states)))
    for load in loads:
        load.wait()
    for r in range(nblk):
        total = jnp.sum(bw_ref[r, 0], axis=1, keepdims=True)
        for k in range(1, kb):
            total = total + jnp.sum(bw_ref[r, k], axis=1, keepdims=True)
        scale = leave_col[r * block:(r + 1) * block, :] / total
        for c in range(nblk):
            acc = bw_ref[r, 0] * jnp.where(cols_ref[0, r] == c, 1.0, 0.0)
            for k in range(1, kb):
                acc = acc + bw_ref[r, k] * jnp.where(cols_ref[k, r] == c, 1.0, 0.0)
            acc = acc * scale
            hi, lo = split(acc)
            rs = slice(r * block, (r + 1) * block)
            cs = slice(c * block, (c + 1) * block)
            w_ref[rs, cs] = acc
            w_hi[rs, cs] = hi
            w_lo[rs, cs] = lo

    em = em_ref[...]
    em = em / jnp.sum(em, axis=0, keepdims=True)
    e_ref[...] = jnp.zeros_like(e_ref)
    for j in range(per):
        for g in range(SUBS):
            s = sym_ref[g * per + j]
            row = jnp.zeros((1, states), f32)
            for v in range(symbols):
                row = row + em[v:v + 1] * jnp.where(s == v, 1.0, 0.0)
            e_ref[j, g:g + 1, :] = row

    eye = (lax.broadcasted_iota(jnp.int32, (states, states), 0)
           == lax.broadcasted_iota(jnp.int32, (states, states), 1))
    full_step = jnp.where(eye, jnp.broadcast_to(stay, (states, states)), 0.0) + w_ref[...]
    for g in range(SUBS):
        x_ref[g] = full_step * e_ref[0, g:g + 1, :]

    def advance(j, carry):
        for g in range(SUBS):
            x = x_ref[g]
            xb = x.astype(bf16)
            acc = dot(xb, w_hi[...]) + dot(xb, w_lo[...])
            x_ref[g] = (x * stay + acc) * e_ref[j, g:g + 1, :]
        return carry

    lax.fori_loop(1, per, advance, 0)

    for g in range(SUBS):
        x = x_ref[g]
        x = x * (1.0 / jnp.max(x))
        hi, lo = split(x)
        p_hi[g] = hi
        p_lo[g] = lo

    def joined(a, b):
        return dot(a[0], b[0]) + (dot(a[0], b[1]) + dot(a[1], b[0]))

    left = joined((p_hi[0], p_lo[0]), (p_hi[1], p_lo[1]))
    x_ref[0] = left
    right = joined((p_hi[2], p_lo[2]), (p_hi[3], p_lo[3]))
    x_ref[1] = right
    whole = joined(split(x_ref[0]), split(x_ref[1]))
    mine[...] = whole * (1.0 / jnp.max(whole))

    inner = jnp.logical_and(chip > 0, chip < chips - 1)

    @pl.when(inner)
    def _():
        pl.semaphore_wait(barrier, 5)

    @pl.when(jnp.logical_not(inner))
    def _():
        pl.semaphore_wait(barrier, 3)

    give_cols = pltpu.make_async_remote_copy(
        src_ref=mine.at[:, half:], dst_ref=got_cols, send_sem=x_send, recv_sem=x_recv,
        device_id={"tm": partner})
    give_rows = pltpu.make_async_remote_copy(
        src_ref=mine.at[:half, :], dst_ref=got_rows, send_sem=x_send, recv_sem=x_recv,
        device_id={"tm": partner})

    @pl.when(core == 0)
    def _():
        give_cols.start()

    @pl.when(core == 1)
    def _():
        give_rows.start()

    hi, lo = split(mine[...])
    h_hi[...] = hi
    h_lo[...] = lo

    @pl.when(core == 0)
    def _():
        give_rows.wait_recv()
        got = split(got_rows[...])
        hi, lo = split(joined((h_hi[:, :half], h_lo[:, :half]), got))
        q_hi[...] = hi
        q_lo[...] = lo

    @pl.when(core == 1)
    def _():
        give_cols.wait_recv()
        got = split(got_cols[...])
        hi, lo = split(joined(got, (h_hi[half:, :], h_lo[half:, :])))
        q_hi[...] = hi
        q_lo[...] = lo

    f_copies = [pltpu.make_async_remote_copy(
        src_ref=f_out, dst_ref=f_in.at[core], send_sem=f_send.at[c], recv_sem=f_recv.at[core],
        device_id={"tm": above + c}) for c in range(2)]
    b_copies = [pltpu.make_async_remote_copy(
        src_ref=b_out, dst_ref=b_in.at[core], send_sem=b_send.at[c], recv_sem=b_recv.at[core],
        device_id={"tm": below + c}) for c in range(2)]
    f_got = [pltpu.make_async_remote_copy(
        src_ref=f_out, dst_ref=f_in.at[c], send_sem=f_send.at[c], recv_sem=f_recv.at[c],
        device_id={"tm": above + c}) for c in range(2)]
    b_got = [pltpu.make_async_remote_copy(
        src_ref=b_out, dst_ref=b_in.at[c], send_sem=b_send.at[c], recv_sem=b_recv.at[c],
        device_id={"tm": below + c}) for c in range(2)]
    give_f = pltpu.make_async_remote_copy(
        src_ref=side_out, dst_ref=f_side, send_sem=s_send, recv_sem=s_recv,
        device_id={"tm": partner})
    give_b = pltpu.make_async_remote_copy(
        src_ref=side_out, dst_ref=b_side, send_sem=s_send, recv_sem=s_recv,
        device_id={"tm": partner})

    def forward_hop():
        @pl.when(chip == 0)
        def _():
            f_in[0] = init_ref[...]
            f_in[1] = jnp.zeros((1, states), f32)

        @pl.when(chip > 0)
        def _():
            for got in f_got:
                got.wait_recv()

        @pl.when(chip < chips - 1)
        def _():
            v = f_in[0] + f_in[1]
            out = thin(jnp.broadcast_to(v, (8, states)), q_hi[...], q_lo[...])
            f_out[...] = out[0:1] * (1.0 / jnp.sum(v))
            for copy in f_copies:
                copy.start()

        @pl.when(core == 0)
        def _():
            v = f_in[0] + f_in[1]
            out = thin(jnp.broadcast_to(v, (8, states)), h_hi[...], h_lo[...])
            side_out[...] = out[0:1] * (1.0 / jnp.sum(v))
            give_f.start()

    def backward_hop():
        @pl.when(chip == chips - 1)
        def _():
            b_in[0] = jnp.full((1, states), 1.0 / states, f32)
            b_in[1] = jnp.zeros((1, states), f32)

        @pl.when(chip < chips - 1)
        def _():
            for got in b_got:
                got.wait_recv()

        @pl.when(chip > 0)
        def _():
            w = b_in[0] + b_in[1]
            out = thin(jnp.broadcast_to(w, (8, states)), q_hi[...], q_lo[...], NT)
            b_out[...] = out[0:1] * (1.0 / jnp.sum(w))
            for copy in b_copies:
                copy.start()

        @pl.when(core == 1)
        def _():
            w = b_in[0] + b_in[1]
            out = thin(jnp.broadcast_to(w, (8, states)), h_hi[...], h_lo[...], NT)
            side_out[...] = out[0:1] * (1.0 / jnp.sum(w))
            give_b.start()

    @pl.when(2 * chip < chips)
    def _():
        forward_hop()
        backward_hop()

    @pl.when(2 * chip >= chips)
    def _():
        backward_hop()
        forward_hop()

    @pl.when(core == 0)
    def _():
        f_side[...] = f_in[0] + f_in[1]
        give_b.wait_recv()

    @pl.when(core == 1)
    def _():
        b_side[...] = b_in[0] + b_in[1]
        give_f.wait_recv()

    def unit(x):
        return x * (1.0 / jnp.sum(x, axis=1, keepdims=True))

    fs = [unit(f_side[...])]
    for g in range(SUBS - 1):
        nxt = thin(jnp.broadcast_to(fs[-1], (8, states)), p_hi[g], p_lo[g])
        fs.append(unit(nxt[0:1]))
    bs = [unit(b_side[...])]
    for g in range(SUBS - 1, 0, -1):
        nxt = thin(jnp.broadcast_to(bs[-1], (8, states)), p_hi[g], p_lo[g], NT)
        bs.append(unit(nxt[0:1]))
    bs = bs[::-1]
    pad = [jnp.zeros((8 - SUBS, states), f32)]
    f = jnp.concatenate(fs + pad, axis=0)
    b = jnp.concatenate(bs + pad, axis=0)
    b_ref[per - 1] = b
    for i in range(per):
        f = (f * stay + thin(f, w_hi[...], w_lo[...])) * e_ref[i]
        u_ref[i] = f
        j = per - 1 - i
        if j > 0:
            m = b * e_ref[j]
            b = m * stay + thin(m, w_hi[...], w_lo[...], NT)
            b_ref[j - 1] = b

    l_ref[...] = jnp.zeros_like(l_ref)
    before = jnp.ones((8, 1), f32)
    for i in range(per):
        u = u_ref[i]
        here = jnp.sum(u, axis=1, keepdims=True)
        logs = jnp.log(here / before)
        before = here
        bb = b_ref[i]
        joint = (u / here) * (bb / jnp.sum(bb, axis=1, keepdims=True))
        occ = states * joint / jnp.sum(joint, axis=1, keepdims=True)
        for g in range(SUBS):
            occ_ref[g * per + i:g * per + i + 1, :] = occ[g:g + 1]
            l_ref[g * per + i:g * per + i + 1, :] = jnp.broadcast_to(logs[g:g + 1], (1, 128))

    ln_ref[...] = jnp.transpose(l_ref[...])[0:1, :steps]

    @pl.when(chip < chips - 1)
    def _():
        for copy in f_copies:
            copy.wait_send()

    @pl.when(chip > 0)
    def _():
        for copy in b_copies:
            copy.wait_send()

    @pl.when(core == 0)
    def _():
        give_cols.wait_send()
        give_f.wait_send()

    @pl.when(core == 1)
    def _():
        give_rows.wait_send()
        give_b.wait_send()


def body(initial_weights, leave_rate, block_weights, block_cols, emission_weights, symbols):
    states = leave_rate.shape[0]
    steps = symbols.shape[0]
    per = steps // SUBS
    vmem = pl.BlockSpec(memory_space=pltpu.VMEM)
    far = pl.BlockSpec(memory_space=pltpu.HBM)
    dma = pltpu.SemaphoreType.DMA
    tall = -(-steps // 128) * 128
    square = (states, states)
    row = pltpu.VMEM((1, states), f32)
    pair = pltpu.VMEM((2, 1, states), f32)
    occupancy, log_norm = pl.pallas_call(
        kernel,
        out_shape=(jax.ShapeDtypeStruct((steps, states), f32),
                   jax.ShapeDtypeStruct((1, steps), f32)),
        in_specs=[vmem, vmem, far, far, far, far],
        out_specs=(vmem, vmem),
        scratch_shapes=[
            pltpu.VMEM(block_weights.shape, f32), pltpu.SMEM(block_cols.shape[::-1], jnp.int32),
            pltpu.VMEM(emission_weights.shape, f32), pltpu.SMEM(symbols.shape, jnp.int32), dma((4,)),
            pltpu.VMEM(square, f32), pltpu.VMEM(square, bf16), pltpu.VMEM(square, bf16),
            pltpu.VMEM((SUBS,) + square, f32),
            pltpu.VMEM((SUBS,) + square, bf16), pltpu.VMEM((SUBS,) + square, bf16),
            pltpu.VMEM(square, bf16), pltpu.VMEM(square, bf16),
            pltpu.VMEM(square, bf16), pltpu.VMEM(square, bf16),
            pltpu.VMEM((per, 8, states), f32), pltpu.VMEM((per, 8, states), f32),
            pltpu.VMEM((per, 8, states), f32), pltpu.VMEM((tall, 128), f32),
            pltpu.VMEM(square, f32), pltpu.VMEM((states, states // 2), f32),
            pltpu.VMEM((states // 2, states), f32),
            pair, row, pair, row, row, row, row,
            dma, dma, dma((2,)), dma((2,)), dma((2,)), dma((2,)), dma, dma,
        ],
        compiler_params=pltpu.CompilerParams(
            collective_id=0, has_side_effects=True, vmem_limit_bytes=48 * 1024 * 1024),
    )(initial_weights[None, :], leave_rate[None, :], block_weights, block_cols.T,
      emission_weights, symbols)
    return occupancy, log_norm[0]


def solution(mesh):
    placed = (P(), P(), P(), P(), P(), P(("grp", "tm")))
    return jax.shard_map(
        body,
        mesh=mesh,
        in_specs=placed,
        out_specs=(P(("grp", "tm"), None), P(("grp", "tm"))),
        check_vma=False,
    )
```

```python
import functools
import jax
import jax.numpy as jnp
from jax import lax
from jax.experimental import pallas as pl
from jax.experimental.pallas import tpu as pltpu
from jax.sharding import PartitionSpec as P

f32 = jnp.float32
bf16 = jnp.bfloat16
SUBS = 4
NN = (((1,), (0,)), ((), ()))


def split(x):
    hi = x.astype(bf16)
    return hi, (x - hi.astype(f32)).astype(bf16)


def dot(a, b):
    return lax.dot_general(a, b, NN, preferred_element_type=f32)


def thin(x, hi, lo):
    top = x.astype(bf16).astype(f32)
    both = jnp.concatenate([top, x - top], axis=0).astype(bf16)
    first = dot(both, hi)
    second = dot(both, lo)
    return first[:8] + (first[8:] + second[:8])


def kernel(init_ref, leave_ref, bw_hbm, cols_hbm, em_hbm, sym_hbm, occ_ref, ln_ref,
           bw_ref, cols_ref, em_ref, sym_ref, in_sems,
           w_ref, w_hi, w_lo, x_ref, p_hi, p_lo, h_hi, h_lo, q_hi, q_lo,
           wt_hi, wt_lo, pt_hi, pt_lo, ht_hi, ht_lo, qt_hi, qt_lo, e_ref, u_ref, b_ref, l_ref,
           mine, got_cols, got_rows, f_in, f_out, b_in, b_out, f_side, b_side, side_out,
           x_send, x_recv, f_send, f_recv, b_send, b_recv, s_send, s_recv):
    pos = lax.axis_index("tm")
    count = lax.axis_size("tm")
    chips = count // 2
    chip = lax.div(pos, 2)
    core = lax.rem(pos, 2)
    partner = chip * 2 + (1 - core)
    below = lax.rem(chip + chips - 1, chips) * 2
    above = lax.rem(chip + 1, chips) * 2
    nblk, kb, block, _ = bw_ref.shape
    states = nblk * block
    symbols = em_ref.shape[0]
    steps = occ_ref.shape[0]
    per = steps // SUBS
    half = states // 2

    loads = [pltpu.make_async_copy(src, dst, in_sems.at[i]) for i, (src, dst) in enumerate(
        [(bw_hbm, bw_ref), (cols_hbm, cols_ref), (em_hbm, em_ref), (sym_hbm, sym_ref)])]
    for load in loads:
        load.start()

    barrier = pltpu.get_barrier_semaphore()

    pl.semaphore_signal(barrier, inc=1, device_id={"tm": partner})

    @pl.when(chip > 0)
    def _():
        for c in range(2):
            pl.semaphore_signal(barrier, inc=1, device_id={"tm": below + c})

    @pl.when(chip < chips - 1)
    def _():
        for c in range(2):
            pl.semaphore_signal(barrier, inc=1, device_id={"tm": above + c})

    leave = leave_ref[...]
    stay = 1.0 - leave
    leave_col = jnp.transpose(jnp.broadcast_to(leave, (128, states)))
    for load in loads:
        load.wait()
    for r in range(nblk):
        total = jnp.sum(bw_ref[r, 0], axis=1, keepdims=True)
        for k in range(1, kb):
            total = total + jnp.sum(bw_ref[r, k], axis=1, keepdims=True)
        scale = leave_col[r * block:(r + 1) * block, :] / total
        for c in range(nblk):
            acc = bw_ref[r, 0] * jnp.where(cols_ref[0, r] == c, 1.0, 0.0)
            for k in range(1, kb):
                acc = acc + bw_ref[r, k] * jnp.where(cols_ref[k, r] == c, 1.0, 0.0)
            acc = acc * scale
            hi, lo = split(acc)
            rs = slice(r * block, (r + 1) * block)
            cs = slice(c * block, (c + 1) * block)
            w_ref[rs, cs] = acc
            w_hi[rs, cs] = hi
            w_lo[rs, cs] = lo

    em = em_ref[...]
    em = em / jnp.sum(em, axis=0, keepdims=True)
    e_ref[...] = jnp.zeros_like(e_ref)
    for j in range(per):
        for g in range(SUBS):
            s = sym_ref[g * per + j]
            row = jnp.zeros((1, states), f32)
            for v in range(symbols):
                row = row + em[v:v + 1] * jnp.where(s == v, 1.0, 0.0)
            e_ref[j, g:g + 1, :] = row

    eye = (lax.broadcasted_iota(jnp.int32, (states, states), 0)
           == lax.broadcasted_iota(jnp.int32, (states, states), 1))
    full_step = jnp.where(eye, jnp.broadcast_to(stay, (states, states)), 0.0) + w_ref[...]
    for g in range(SUBS):
        x_ref[g] = full_step * e_ref[0, g:g + 1, :]

    def advance(j, carry):
        for g in range(SUBS):
            x = x_ref[g]
            xb = x.astype(bf16)
            acc = dot(xb, w_hi[...]) + dot(xb, w_lo[...])
            x_ref[g] = (x * stay + acc) * e_ref[j, g:g + 1, :]
        return carry

    lax.fori_loop(1, per, advance, 0)

    for g in range(SUBS):
        x = x_ref[g]
        x = x * (1.0 / jnp.max(x))
        hi, lo = split(x)
        p_hi[g] = hi
        p_lo[g] = lo

    def joined(a, b):
        return dot(a[0], b[0]) + (dot(a[0], b[1]) + dot(a[1], b[0]))

    left = joined((p_hi[0], p_lo[0]), (p_hi[1], p_lo[1]))
    x_ref[SUBS] = left
    right = joined((p_hi[2], p_lo[2]), (p_hi[3], p_lo[3]))
    x_ref[SUBS + 1] = right
    whole = joined(split(x_ref[SUBS]), split(x_ref[SUBS + 1]))
    mine[...] = whole * (1.0 / jnp.max(whole))

    inner = jnp.logical_and(chip > 0, chip < chips - 1)

    @pl.when(inner)
    def _():
        pl.semaphore_wait(barrier, 5)

    @pl.when(jnp.logical_not(inner))
    def _():
        pl.semaphore_wait(barrier, 3)

    give_cols = pltpu.make_async_remote_copy(
        src_ref=mine.at[:, half:], dst_ref=got_cols, send_sem=x_send, recv_sem=x_recv,
        device_id={"tm": partner})
    give_rows = pltpu.make_async_remote_copy(
        src_ref=mine.at[:half, :], dst_ref=got_rows, send_sem=x_send, recv_sem=x_recv,
        device_id={"tm": partner})

    @pl.when(core == 0)
    def _():
        give_cols.start()

    @pl.when(core == 1)
    def _():
        give_rows.start()

    hi, lo = split(mine[...])
    h_hi[...] = hi
    h_lo[...] = lo
    hi, lo = split(jnp.transpose(w_ref[...]))
    wt_hi[...] = hi
    wt_lo[...] = lo
    for g in range(1, SUBS):
        hi, lo = split(jnp.transpose(x_ref[g]))
        pt_hi[g] = hi
        pt_lo[g] = lo

    @pl.when(core == 1)
    def _():
        hi, lo = split(jnp.transpose(mine[...]))
        ht_hi[...] = hi
        ht_lo[...] = lo

    @pl.when(core == 0)
    def _():
        give_rows.wait_recv()
        got = split(got_rows[...])
        x_ref[SUBS] = joined((h_hi[:, :half], h_lo[:, :half]), got)

    @pl.when(core == 1)
    def _():
        give_cols.wait_recv()
        got = split(got_cols[...])
        x_ref[SUBS] = joined(got, (h_hi[half:, :], h_lo[half:, :]))

    hi, lo = split(x_ref[SUBS])
    q_hi[...] = hi
    q_lo[...] = lo
    hi, lo = split(jnp.transpose(x_ref[SUBS]))
    qt_hi[...] = hi
    qt_lo[...] = lo

    f_copies = [pltpu.make_async_remote_copy(
        src_ref=f_out, dst_ref=f_in.at[core], send_sem=f_send.at[c], recv_sem=f_recv.at[core],
        device_id={"tm": above + c}) for c in range(2)]
    b_copies = [pltpu.make_async_remote_copy(
        src_ref=b_out, dst_ref=b_in.at[core], send_sem=b_send.at[c], recv_sem=b_recv.at[core],
        device_id={"tm": below + c}) for c in range(2)]
    f_got = [pltpu.make_async_remote_copy(
        src_ref=f_out, dst_ref=f_in.at[c], send_sem=f_send.at[c], recv_sem=f_recv.at[c],
        device_id={"tm": above + c}) for c in range(2)]
    b_got = [pltpu.make_async_remote_copy(
        src_ref=b_out, dst_ref=b_in.at[c], send_sem=b_send.at[c], recv_sem=b_recv.at[c],
        device_id={"tm": below + c}) for c in range(2)]
    give_f = pltpu.make_async_remote_copy(
        src_ref=side_out, dst_ref=f_side, send_sem=s_send, recv_sem=s_recv,
        device_id={"tm": partner})
    give_b = pltpu.make_async_remote_copy(
        src_ref=side_out, dst_ref=b_side, send_sem=s_send, recv_sem=s_recv,
        device_id={"tm": partner})

    def forward_hop():
        @pl.when(chip == 0)
        def _():
            f_in[0] = init_ref[...]
            f_in[1] = jnp.zeros((1, states), f32)

        @pl.when(chip > 0)
        def _():
            for got in f_got:
                got.wait_recv()

        @pl.when(chip < chips - 1)
        def _():
            v = f_in[0] + f_in[1]
            out = thin(jnp.broadcast_to(v, (8, states)), q_hi[...], q_lo[...])
            f_out[...] = out[0:1] * (1.0 / jnp.sum(v))
            for copy in f_copies:
                copy.start()

        @pl.when(core == 0)
        def _():
            v = f_in[0] + f_in[1]
            out = thin(jnp.broadcast_to(v, (8, states)), h_hi[...], h_lo[...])
            side_out[...] = out[0:1] * (1.0 / jnp.sum(v))
            give_f.start()

    def backward_hop():
        @pl.when(chip == chips - 1)
        def _():
            b_in[0] = jnp.full((1, states), 1.0 / states, f32)
            b_in[1] = jnp.zeros((1, states), f32)

        @pl.when(chip < chips - 1)
        def _():
            for got in b_got:
                got.wait_recv()

        @pl.when(chip > 0)
        def _():
            w = b_in[0] + b_in[1]
            out = thin(jnp.broadcast_to(w, (8, states)), qt_hi[...], qt_lo[...])
            b_out[...] = out[0:1] * (1.0 / jnp.sum(w))
            for copy in b_copies:
                copy.start()

        @pl.when(core == 1)
        def _():
            w = b_in[0] + b_in[1]
            out = thin(jnp.broadcast_to(w, (8, states)), ht_hi[...], ht_lo[...])
            side_out[...] = out[0:1] * (1.0 / jnp.sum(w))
            give_b.start()

    @pl.when(2 * chip < chips)
    def _():
        forward_hop()
        backward_hop()

    @pl.when(2 * chip >= chips)
    def _():
        backward_hop()
        forward_hop()

    @pl.when(core == 0)
    def _():
        f_side[...] = f_in[0] + f_in[1]
        give_b.wait_recv()

    @pl.when(core == 1)
    def _():
        b_side[...] = b_in[0] + b_in[1]
        give_f.wait_recv()

    def unit(x):
        return x * (1.0 / jnp.sum(x, axis=1, keepdims=True))

    fs = [unit(f_side[...])]
    for g in range(SUBS - 1):
        nxt = thin(jnp.broadcast_to(fs[-1], (8, states)), p_hi[g], p_lo[g])
        fs.append(unit(nxt[0:1]))
    bs = [unit(b_side[...])]
    for g in range(SUBS - 1, 0, -1):
        nxt = thin(jnp.broadcast_to(bs[-1], (8, states)), pt_hi[g], pt_lo[g])
        bs.append(unit(nxt[0:1]))
    bs = bs[::-1]
    pad = [jnp.zeros((8 - SUBS, states), f32)]
    f = jnp.concatenate(fs + pad, axis=0)
    b = jnp.concatenate(bs + pad, axis=0)
    b_ref[per - 1] = b
    for i in range(per):
        f = (f * stay + thin(f, w_hi[...], w_lo[...])) * e_ref[i]
        u_ref[i] = f
        j = per - 1 - i
        if j > 0:
            m = b * e_ref[j]
            b = m * stay + thin(m, wt_hi[...], wt_lo[...])
            b_ref[j - 1] = b

    l_ref[...] = jnp.zeros_like(l_ref)
    before = jnp.ones((8, 1), f32)
    for i in range(per):
        u = u_ref[i]
        here = jnp.sum(u, axis=1, keepdims=True)
        logs = jnp.log(here / before)
        before = here
        bb = b_ref[i]
        joint = (u / here) * (bb / jnp.sum(bb, axis=1, keepdims=True))
        occ = states * joint / jnp.sum(joint, axis=1, keepdims=True)
        for g in range(SUBS):
            occ_ref[g * per + i:g * per + i + 1, :] = occ[g:g + 1]
            l_ref[g * per + i:g * per + i + 1, :] = jnp.broadcast_to(logs[g:g + 1], (1, 128))

    ln_ref[...] = jnp.transpose(l_ref[...])[0:1, :steps]

    @pl.when(chip < chips - 1)
    def _():
        for copy in f_copies:
            copy.wait_send()

    @pl.when(chip > 0)
    def _():
        for copy in b_copies:
            copy.wait_send()

    @pl.when(core == 0)
    def _():
        give_cols.wait_send()
        give_f.wait_send()

    @pl.when(core == 1)
    def _():
        give_rows.wait_send()
        give_b.wait_send()


def body(initial_weights, leave_rate, block_weights, block_cols, emission_weights, symbols):
    states = leave_rate.shape[0]
    steps = symbols.shape[0]
    per = steps // SUBS
    vmem = pl.BlockSpec(memory_space=pltpu.VMEM)
    far = pl.BlockSpec(memory_space=pltpu.HBM)
    dma = pltpu.SemaphoreType.DMA
    tall = -(-steps // 128) * 128
    square = (states, states)
    row = pltpu.VMEM((1, states), f32)
    pair = pltpu.VMEM((2, 1, states), f32)
    occupancy, log_norm = pl.pallas_call(
        kernel,
        out_shape=(jax.ShapeDtypeStruct((steps, states), f32),
                   jax.ShapeDtypeStruct((1, steps), f32)),
        in_specs=[vmem, vmem, far, far, far, far],
        out_specs=(vmem, vmem),
        scratch_shapes=[
            pltpu.VMEM(block_weights.shape, f32), pltpu.SMEM(block_cols.shape[::-1], jnp.int32),
            pltpu.VMEM(emission_weights.shape, f32), pltpu.SMEM(symbols.shape, jnp.int32), dma((4,)),
            pltpu.VMEM(square, f32), pltpu.VMEM(square, bf16), pltpu.VMEM(square, bf16),
            pltpu.VMEM((SUBS + 2,) + square, f32),
            pltpu.VMEM((SUBS,) + square, bf16), pltpu.VMEM((SUBS,) + square, bf16),
            pltpu.VMEM(square, bf16), pltpu.VMEM(square, bf16),
            pltpu.VMEM(square, bf16), pltpu.VMEM(square, bf16),
            pltpu.VMEM(square, bf16), pltpu.VMEM(square, bf16),
            pltpu.VMEM((SUBS,) + square, bf16), pltpu.VMEM((SUBS,) + square, bf16),
            pltpu.VMEM(square, bf16), pltpu.VMEM(square, bf16),
            pltpu.VMEM(square, bf16), pltpu.VMEM(square, bf16),
            pltpu.VMEM((per, 8, states), f32), pltpu.VMEM((per, 8, states), f32),
            pltpu.VMEM((per, 8, states), f32), pltpu.VMEM((tall, 128), f32),
            pltpu.VMEM(square, f32), pltpu.VMEM((states, states // 2), f32),
            pltpu.VMEM((states // 2, states), f32),
            pair, row, pair, row, row, row, row,
            dma, dma, dma((2,)), dma((2,)), dma((2,)), dma((2,)), dma, dma,
        ],
        compiler_params=pltpu.CompilerParams(
            collective_id=0, has_side_effects=True, vmem_limit_bytes=64 * 1024 * 1024 - 65536),
    )(initial_weights[None, :], leave_rate[None, :], block_weights, block_cols.T,
      emission_weights, symbols)
    return occupancy, log_norm[0]


def solution(mesh):
    placed = (P(), P(), P(), P(), P(), P(("grp", "tm")))
    return jax.shard_map(
        body,
        mesh=mesh,
        in_specs=placed,
        out_specs=(P(("grp", "tm"), None), P(("grp", "tm"))),
        check_vma=False,
    )
```

```python
import functools
import jax
import jax.numpy as jnp
from jax import lax
from jax.experimental import pallas as pl
from jax.experimental.pallas import tpu as pltpu
from jax.sharding import PartitionSpec as P

f32 = jnp.float32
bf16 = jnp.bfloat16
SUBS = 4
NN = (((1,), (0,)), ((), ()))


def split(x):
    hi = x.astype(bf16)
    return hi, (x - hi.astype(f32)).astype(bf16)


def dot(a, b):
    return lax.dot_general(a, b, NN, preferred_element_type=f32)


def thin(x, hi, lo):
    top = x.astype(bf16).astype(f32)
    both = jnp.concatenate([top, x - top], axis=0).astype(bf16)
    first = dot(both, hi)
    second = dot(both, lo)
    return first[:8] + (first[8:] + second[:8])


def kernel(init_ref, leave_ref, bw_hbm, cols_hbm, em_hbm, sym_hbm, occ_ref, ln_ref,
           bw_ref, cols_ref, em_ref, sym_ref, in_sems,
           w_ref, w_hi, w_lo, x_ref, p_hi, p_lo, h_hi, h_lo, q_hi, q_lo,
           wt_hi, wt_lo, pt_hi, pt_lo, ht_hi, ht_lo, qt_hi, qt_lo, e_ref, u_ref, b_ref, l_ref,
           mine, got_cols, got_rows, f_in, f_out, b_in, b_out, f_side, b_side, side_out,
           x_send, x_recv, f_send, f_recv, b_send, b_recv, s_send, s_recv):
    pos = lax.axis_index("tm")
    count = lax.axis_size("tm")
    chips = count // 2
    chip = lax.div(pos, 2)
    core = lax.rem(pos, 2)
    partner = chip * 2 + (1 - core)
    below = lax.rem(chip + chips - 1, chips) * 2
    above = lax.rem(chip + 1, chips) * 2
    nblk, kb, block, _ = bw_ref.shape
    states = nblk * block
    symbols = em_ref.shape[0]
    steps = occ_ref.shape[0]
    per = steps // SUBS
    half = states // 2

    loads = [pltpu.make_async_copy(src, dst, in_sems.at[i]) for i, (src, dst) in enumerate(
        [(bw_hbm, bw_ref), (cols_hbm, cols_ref), (em_hbm, em_ref), (sym_hbm, sym_ref)])]
    for load in loads:
        load.start()

    barrier = pltpu.get_barrier_semaphore()

    pl.semaphore_signal(barrier, inc=1, device_id={"tm": partner})

    @pl.when(chip > 0)
    def _():
        for c in range(2):
            pl.semaphore_signal(barrier, inc=1, device_id={"tm": below + c})

    @pl.when(chip < chips - 1)
    def _():
        for c in range(2):
            pl.semaphore_signal(barrier, inc=1, device_id={"tm": above + c})

    leave = leave_ref[...]
    stay = 1.0 - leave
    leave_col = jnp.transpose(jnp.broadcast_to(leave, (128, states)))
    for load in loads:
        load.wait()
    for r in range(nblk):
        total = jnp.sum(bw_ref[r, 0], axis=1, keepdims=True)
        for k in range(1, kb):
            total = total + jnp.sum(bw_ref[r, k], axis=1, keepdims=True)
        scale = leave_col[r * block:(r + 1) * block, :] / total
        for c in range(nblk):
            acc = bw_ref[r, 0] * jnp.where(cols_ref[0, r] == c, 1.0, 0.0)
            for k in range(1, kb):
                acc = acc + bw_ref[r, k] * jnp.where(cols_ref[k, r] == c, 1.0, 0.0)
            acc = acc * scale
            hi, lo = split(acc)
            rs = slice(r * block, (r + 1) * block)
            cs = slice(c * block, (c + 1) * block)
            w_ref[rs, cs] = acc
            w_hi[rs, cs] = hi
            w_lo[rs, cs] = lo

    em = em_ref[...]
    em = em / jnp.sum(em, axis=0, keepdims=True)
    e_ref[...] = jnp.zeros_like(e_ref)
    for j in range(per):
        for g in range(SUBS):
            s = sym_ref[g * per + j]
            row = jnp.zeros((1, states), f32)
            for v in range(symbols):
                row = row + em[v:v + 1] * jnp.where(s == v, 1.0, 0.0)
            e_ref[j, g:g + 1, :] = row

    eye = (lax.broadcasted_iota(jnp.int32, (states, states), 0)
           == lax.broadcasted_iota(jnp.int32, (states, states), 1))
    full_step = jnp.where(eye, jnp.broadcast_to(stay, (states, states)), 0.0) + w_ref[...]
    for g in range(SUBS):
        x_ref[g] = full_step * e_ref[0, g:g + 1, :]

    def advance(j, low):
        for g in range(SUBS):
            x = x_ref[g]
            xb = x.astype(bf16)
            acc = dot(xb, w_hi[...])
            if low:
                acc = acc + low * dot(xb, w_lo[...])
            x_ref[g] = (x * stay + acc) * e_ref[j, g:g + 1, :]

    pairs = max(per - 2, 0) // 2

    def advance_pair(i, carry):
        advance(2 * i + 1, 0)
        advance(2 * i + 2, 2.0)
        return carry

    lax.fori_loop(0, pairs, advance_pair, 0)
    for j in range(2 * pairs + 1, per):
        advance(j, 1.0)

    for g in range(SUBS):
        x = x_ref[g]
        x = x * (1.0 / jnp.max(x))
        hi, lo = split(x)
        p_hi[g] = hi
        p_lo[g] = lo

    def joined(a, b):
        return dot(a[0], b[0]) + (dot(a[0], b[1]) + dot(a[1], b[0]))

    left = joined((p_hi[0], p_lo[0]), (p_hi[1], p_lo[1]))
    x_ref[SUBS] = left
    right = joined((p_hi[2], p_lo[2]), (p_hi[3], p_lo[3]))
    x_ref[SUBS + 1] = right
    whole = joined(split(x_ref[SUBS]), split(x_ref[SUBS + 1]))
    mine[...] = whole * (1.0 / jnp.max(whole))

    inner = jnp.logical_and(chip > 0, chip < chips - 1)

    @pl.when(inner)
    def _():
        pl.semaphore_wait(barrier, 5)

    @pl.when(jnp.logical_not(inner))
    def _():
        pl.semaphore_wait(barrier, 3)

    give_cols = pltpu.make_async_remote_copy(
        src_ref=mine.at[:, half:], dst_ref=got_cols, send_sem=x_send, recv_sem=x_recv,
        device_id={"tm": partner})
    give_rows = pltpu.make_async_remote_copy(
        src_ref=mine.at[:half, :], dst_ref=got_rows, send_sem=x_send, recv_sem=x_recv,
        device_id={"tm": partner})

    @pl.when(core == 0)
    def _():
        give_cols.start()

    @pl.when(core == 1)
    def _():
        give_rows.start()

    hi, lo = split(mine[...])
    h_hi[...] = hi
    h_lo[...] = lo
    hi, lo = split(jnp.transpose(w_ref[...]))
    wt_hi[...] = hi
    wt_lo[...] = lo
    for g in range(1, SUBS):
        hi, lo = split(jnp.transpose(x_ref[g]))
        pt_hi[g] = hi
        pt_lo[g] = lo

    @pl.when(core == 1)
    def _():
        hi, lo = split(jnp.transpose(mine[...]))
        ht_hi[...] = hi
        ht_lo[...] = lo

    @pl.when(core == 0)
    def _():
        give_rows.wait_recv()
        got = split(got_rows[...])
        x_ref[SUBS] = joined((h_hi[:, :half], h_lo[:, :half]), got)

    @pl.when(core == 1)
    def _():
        give_cols.wait_recv()
        got = split(got_cols[...])
        x_ref[SUBS] = joined(got, (h_hi[half:, :], h_lo[half:, :]))

    hi, lo = split(x_ref[SUBS])
    q_hi[...] = hi
    q_lo[...] = lo
    hi, lo = split(jnp.transpose(x_ref[SUBS]))
    qt_hi[...] = hi
    qt_lo[...] = lo

    f_copies = [pltpu.make_async_remote_copy(
        src_ref=f_out, dst_ref=f_in.at[core], send_sem=f_send.at[c], recv_sem=f_recv.at[core],
        device_id={"tm": above + c}) for c in range(2)]
    b_copies = [pltpu.make_async_remote_copy(
        src_ref=b_out, dst_ref=b_in.at[core], send_sem=b_send.at[c], recv_sem=b_recv.at[core],
        device_id={"tm": below + c}) for c in range(2)]
    f_got = [pltpu.make_async_remote_copy(
        src_ref=f_out, dst_ref=f_in.at[c], send_sem=f_send.at[c], recv_sem=f_recv.at[c],
        device_id={"tm": above + c}) for c in range(2)]
    b_got = [pltpu.make_async_remote_copy(
        src_ref=b_out, dst_ref=b_in.at[c], send_sem=b_send.at[c], recv_sem=b_recv.at[c],
        device_id={"tm": below + c}) for c in range(2)]
    give_f = pltpu.make_async_remote_copy(
        src_ref=side_out, dst_ref=f_side, send_sem=s_send, recv_sem=s_recv,
        device_id={"tm": partner})
    give_b = pltpu.make_async_remote_copy(
        src_ref=side_out, dst_ref=b_side, send_sem=s_send, recv_sem=s_recv,
        device_id={"tm": partner})

    def forward_hop():
        @pl.when(chip == 0)
        def _():
            f_in[0] = init_ref[...]
            f_in[1] = jnp.zeros((1, states), f32)

        @pl.when(chip > 0)
        def _():
            for got in f_got:
                got.wait_recv()

        @pl.when(chip < chips - 1)
        def _():
            v = f_in[0] + f_in[1]
            out = thin(jnp.broadcast_to(v, (8, states)), q_hi[...], q_lo[...])
            f_out[...] = out[0:1] * (1.0 / jnp.sum(v))
            for copy in f_copies:
                copy.start()

        @pl.when(core == 0)
        def _():
            v = f_in[0] + f_in[1]
            out = thin(jnp.broadcast_to(v, (8, states)), h_hi[...], h_lo[...])
            side_out[...] = out[0:1] * (1.0 / jnp.sum(v))
            give_f.start()

    def backward_hop():
        @pl.when(chip == chips - 1)
        def _():
            b_in[0] = jnp.full((1, states), 1.0 / states, f32)
            b_in[1] = jnp.zeros((1, states), f32)

        @pl.when(chip < chips - 1)
        def _():
            for got in b_got:
                got.wait_recv()

        @pl.when(chip > 0)
        def _():
            w = b_in[0] + b_in[1]
            out = thin(jnp.broadcast_to(w, (8, states)), qt_hi[...], qt_lo[...])
            b_out[...] = out[0:1] * (1.0 / jnp.sum(w))
            for copy in b_copies:
                copy.start()

        @pl.when(core == 1)
        def _():
            w = b_in[0] + b_in[1]
            out = thin(jnp.broadcast_to(w, (8, states)), ht_hi[...], ht_lo[...])
            side_out[...] = out[0:1] * (1.0 / jnp.sum(w))
            give_b.start()

    @pl.when(2 * chip < chips)
    def _():
        forward_hop()
        backward_hop()

    @pl.when(2 * chip >= chips)
    def _():
        backward_hop()
        forward_hop()

    @pl.when(core == 0)
    def _():
        f_side[...] = f_in[0] + f_in[1]
        give_b.wait_recv()

    @pl.when(core == 1)
    def _():
        b_side[...] = b_in[0] + b_in[1]
        give_f.wait_recv()

    def unit(x):
        return x * (1.0 / jnp.sum(x, axis=1, keepdims=True))

    fs = [unit(f_side[...])]
    for g in range(SUBS - 1):
        nxt = thin(jnp.broadcast_to(fs[-1], (8, states)), p_hi[g], p_lo[g])
        fs.append(unit(nxt[0:1]))
    bs = [unit(b_side[...])]
    for g in range(SUBS - 1, 0, -1):
        nxt = thin(jnp.broadcast_to(bs[-1], (8, states)), pt_hi[g], pt_lo[g])
        bs.append(unit(nxt[0:1]))
    bs = bs[::-1]
    pad = [jnp.zeros((8 - SUBS, states), f32)]
    f = jnp.concatenate(fs + pad, axis=0)
    b = jnp.concatenate(bs + pad, axis=0)
    b_ref[per - 1] = b
    for i in range(per):
        f = (f * stay + thin(f, w_hi[...], w_lo[...])) * e_ref[i]
        u_ref[i] = f
        j = per - 1 - i
        if j > 0:
            m = b * e_ref[j]
            b = m * stay + thin(m, wt_hi[...], wt_lo[...])
            b_ref[j - 1] = b

    l_ref[...] = jnp.zeros_like(l_ref)
    before = jnp.ones((8, 1), f32)
    for i in range(per):
        u = u_ref[i]
        here = jnp.sum(u, axis=1, keepdims=True)
        logs = jnp.log(here / before)
        before = here
        bb = b_ref[i]
        joint = (u / here) * (bb / jnp.sum(bb, axis=1, keepdims=True))
        occ = states * joint / jnp.sum(joint, axis=1, keepdims=True)
        for g in range(SUBS):
            occ_ref[g * per + i:g * per + i + 1, :] = occ[g:g + 1]
            l_ref[g * per + i:g * per + i + 1, :] = jnp.broadcast_to(logs[g:g + 1], (1, 128))

    ln_ref[...] = jnp.transpose(l_ref[...])[0:1, :steps]

    @pl.when(chip < chips - 1)
    def _():
        for copy in f_copies:
            copy.wait_send()

    @pl.when(chip > 0)
    def _():
        for copy in b_copies:
            copy.wait_send()

    @pl.when(core == 0)
    def _():
        give_cols.wait_send()
        give_f.wait_send()

    @pl.when(core == 1)
    def _():
        give_rows.wait_send()
        give_b.wait_send()


def body(initial_weights, leave_rate, block_weights, block_cols, emission_weights, symbols):
    states = leave_rate.shape[0]
    steps = symbols.shape[0]
    per = steps // SUBS
    vmem = pl.BlockSpec(memory_space=pltpu.VMEM)
    far = pl.BlockSpec(memory_space=pltpu.HBM)
    dma = pltpu.SemaphoreType.DMA
    tall = -(-steps // 128) * 128
    square = (states, states)
    row = pltpu.VMEM((1, states), f32)
    pair = pltpu.VMEM((2, 1, states), f32)
    occupancy, log_norm = pl.pallas_call(
        kernel,
        out_shape=(jax.ShapeDtypeStruct((steps, states), f32),
                   jax.ShapeDtypeStruct((1, steps), f32)),
        in_specs=[vmem, vmem, far, far, far, far],
        out_specs=(vmem, vmem),
        scratch_shapes=[
            pltpu.VMEM(block_weights.shape, f32), pltpu.SMEM(block_cols.shape[::-1], jnp.int32),
            pltpu.VMEM(emission_weights.shape, f32), pltpu.SMEM(symbols.shape, jnp.int32), dma((4,)),
            pltpu.VMEM(square, f32), pltpu.VMEM(square, bf16), pltpu.VMEM(square, bf16),
            pltpu.VMEM((SUBS + 2,) + square, f32),
            pltpu.VMEM((SUBS,) + square, bf16), pltpu.VMEM((SUBS,) + square, bf16),
            pltpu.VMEM(square, bf16), pltpu.VMEM(square, bf16),
            pltpu.VMEM(square, bf16), pltpu.VMEM(square, bf16),
            pltpu.VMEM(square, bf16), pltpu.VMEM(square, bf16),
            pltpu.VMEM((SUBS,) + square, bf16), pltpu.VMEM((SUBS,) + square, bf16),
            pltpu.VMEM(square, bf16), pltpu.VMEM(square, bf16),
            pltpu.VMEM(square, bf16), pltpu.VMEM(square, bf16),
            pltpu.VMEM((per, 8, states), f32), pltpu.VMEM((per, 8, states), f32),
            pltpu.VMEM((per, 8, states), f32), pltpu.VMEM((tall, 128), f32),
            pltpu.VMEM(square, f32), pltpu.VMEM((states, states // 2), f32),
            pltpu.VMEM((states // 2, states), f32),
            pair, row, pair, row, row, row, row,
            dma, dma, dma((2,)), dma((2,)), dma((2,)), dma((2,)), dma, dma,
        ],
        compiler_params=pltpu.CompilerParams(
            collective_id=0, has_side_effects=True, vmem_limit_bytes=64 * 1024 * 1024 - 65536),
    )(initial_weights[None, :], leave_rate[None, :], block_weights, block_cols.T,
      emission_weights, symbols)
    return occupancy, log_norm[0]


def solution(mesh):
    placed = (P(), P(), P(), P(), P(), P(("grp", "tm")))
    return jax.shard_map(
        body,
        mesh=mesh,
        in_specs=placed,
        out_specs=(P(("grp", "tm"), None), P(("grp", "tm"))),
        check_vma=False,
    )
```

```python
import functools
import jax
import jax.numpy as jnp
from jax import lax
from jax.experimental import pallas as pl
from jax.experimental.pallas import tpu as pltpu
from jax.sharding import PartitionSpec as P

f32 = jnp.float32
bf16 = jnp.bfloat16
SUBS = 4
NN = (((1,), (0,)), ((), ()))


def split(x):
    hi = x.astype(bf16)
    return hi, (x - hi.astype(f32)).astype(bf16)


def dot(a, b):
    return lax.dot_general(a, b, NN, preferred_element_type=f32)


def thin(x, hi, lo):
    top = x.astype(bf16).astype(f32)
    both = jnp.concatenate([top, x - top], axis=0).astype(bf16)
    first = dot(both, hi)
    second = dot(both, lo)
    return first[:8] + (first[8:] + second[:8])


def kernel(init_ref, leave_ref, bw_hbm, cols_hbm, em_hbm, sym_hbm, occ_ref, ln_ref,
           bw_ref, cols_ref, em_ref, sym_ref, in_sems,
           w_ref, w_hi, w_lo, x_ref, p_hi, p_lo, h_hi, h_lo, q_hi, q_lo,
           wt_hi, wt_lo, pt_hi, pt_lo, ht_hi, ht_lo, qt_hi, qt_lo, e_ref, u_ref, b_ref, l_ref,
           mine, got_cols, got_rows, f_in, f_out, b_in, b_out, f_side, b_side, side_out,
           x_send, x_recv, f_send, f_recv, b_send, b_recv, s_send, s_recv):
    pos = lax.axis_index("tm")
    count = lax.axis_size("tm")
    chips = count // 2
    chip = lax.div(pos, 2)
    core = lax.rem(pos, 2)
    partner = chip * 2 + (1 - core)
    below = lax.rem(chip + chips - 1, chips) * 2
    above = lax.rem(chip + 1, chips) * 2
    nblk, kb, block, _ = bw_ref.shape
    states = nblk * block
    symbols = em_ref.shape[0]
    steps = occ_ref.shape[0]
    per = steps // SUBS
    half = states // 2

    loads = [pltpu.make_async_copy(src, dst, in_sems.at[i]) for i, (src, dst) in enumerate(
        [(bw_hbm, bw_ref), (cols_hbm, cols_ref), (em_hbm, em_ref), (sym_hbm, sym_ref)])]
    for load in loads:
        load.start()

    barrier = pltpu.get_barrier_semaphore()

    pl.semaphore_signal(barrier, inc=1, device_id={"tm": partner})

    @pl.when(chip > 0)
    def _():
        for c in range(2):
            pl.semaphore_signal(barrier, inc=1, device_id={"tm": below + c})

    @pl.when(chip < chips - 1)
    def _():
        for c in range(2):
            pl.semaphore_signal(barrier, inc=1, device_id={"tm": above + c})

    leave = leave_ref[...]
    stay = 1.0 - leave
    leave_col = jnp.transpose(jnp.broadcast_to(leave, (128, states)))
    for load in loads:
        load.wait()
    for r in range(nblk):
        total = jnp.sum(bw_ref[r, 0], axis=1, keepdims=True)
        for k in range(1, kb):
            total = total + jnp.sum(bw_ref[r, k], axis=1, keepdims=True)
        scale = leave_col[r * block:(r + 1) * block, :] / total
        for c in range(nblk):
            acc = bw_ref[r, 0] * jnp.where(cols_ref[0, r] == c, 1.0, 0.0)
            for k in range(1, kb):
                acc = acc + bw_ref[r, k] * jnp.where(cols_ref[k, r] == c, 1.0, 0.0)
            acc = acc * scale
            hi, lo = split(acc)
            rs = slice(r * block, (r + 1) * block)
            cs = slice(c * block, (c + 1) * block)
            w_ref[rs, cs] = acc
            w_hi[rs, cs] = hi
            w_lo[rs, cs] = lo

    em = em_ref[...]
    em = em / jnp.sum(em, axis=0, keepdims=True)
    e_ref[...] = jnp.zeros_like(e_ref)
    for j in range(per):
        for g in range(SUBS):
            s = sym_ref[g * per + j]
            row = jnp.zeros((1, states), f32)
            for v in range(symbols):
                row = row + em[v:v + 1] * jnp.where(s == v, 1.0, 0.0)
            e_ref[j, g:g + 1, :] = row

    eye = (lax.broadcasted_iota(jnp.int32, (states, states), 0)
           == lax.broadcasted_iota(jnp.int32, (states, states), 1))
    full_step = jnp.where(eye, jnp.broadcast_to(stay, (states, states)), 0.0) + w_ref[...]
    for g in range(SUBS):
        x_ref[g] = full_step * e_ref[0, g:g + 1, :]

    def advance(j, low):
        for g in range(SUBS):
            x = x_ref[g]
            xb = x.astype(bf16)
            acc = dot(xb, w_hi[...])
            if low:
                acc = acc + low * dot(xb, w_lo[...])
            x_ref[g] = (x * stay + acc) * e_ref[j, g:g + 1, :]

    pairs = max(per - 2, 0) // 2

    def advance_pair(i, carry):
        advance(2 * i + 1, 0)
        advance(2 * i + 2, 2.0)
        return carry

    lax.fori_loop(0, pairs, advance_pair, 0)
    for j in range(2 * pairs + 1, per):
        advance(j, 1.0)

    for g in range(SUBS):
        x = x_ref[g]
        x = x * (1.0 / jnp.max(x))
        hi, lo = split(x)
        p_hi[g] = hi
        p_lo[g] = lo

    def joined(a, b):
        return dot(a[0], b[0]) + (dot(a[0], b[1]) + dot(a[1], b[0]))

    left = joined((p_hi[0], p_lo[0]), (p_hi[1], p_lo[1]))
    x_ref[SUBS] = left
    right = joined((p_hi[2], p_lo[2]), (p_hi[3], p_lo[3]))
    x_ref[SUBS + 1] = right
    whole = joined(split(x_ref[SUBS]), split(x_ref[SUBS + 1]))
    mine[...] = whole * (1.0 / jnp.max(whole))

    inner = jnp.logical_and(chip > 0, chip < chips - 1)

    @pl.when(inner)
    def _():
        pl.semaphore_wait(barrier, 5)

    @pl.when(jnp.logical_not(inner))
    def _():
        pl.semaphore_wait(barrier, 3)

    give_cols = pltpu.make_async_remote_copy(
        src_ref=mine.at[:, half:], dst_ref=got_cols, send_sem=x_send, recv_sem=x_recv,
        device_id={"tm": partner})
    give_rows = pltpu.make_async_remote_copy(
        src_ref=mine.at[:half, :], dst_ref=got_rows, send_sem=x_send, recv_sem=x_recv,
        device_id={"tm": partner})

    @pl.when(core == 0)
    def _():
        give_cols.start()

    @pl.when(core == 1)
    def _():
        give_rows.start()

    hi, lo = split(mine[...])
    h_hi[...] = hi
    h_lo[...] = lo
    hi, lo = split(jnp.transpose(w_ref[...]))
    wt_hi[...] = hi
    wt_lo[...] = lo
    for g in range(1, SUBS):
        hi, lo = split(jnp.transpose(x_ref[g]))
        pt_hi[g] = hi
        pt_lo[g] = lo

    @pl.when(core == 1)
    def _():
        hi, lo = split(jnp.transpose(mine[...]))
        ht_hi[...] = hi
        ht_lo[...] = lo

    @pl.when(core == 0)
    def _():
        give_rows.wait_recv()
        got = split(got_rows[...])
        x_ref[SUBS] = joined((h_hi[:, :half], h_lo[:, :half]), got)

    @pl.when(core == 1)
    def _():
        give_cols.wait_recv()
        got = split(got_cols[...])
        x_ref[SUBS] = joined(got, (h_hi[half:, :], h_lo[half:, :]))

    hi, lo = split(x_ref[SUBS])
    q_hi[...] = hi
    q_lo[...] = lo
    hi, lo = split(jnp.transpose(x_ref[SUBS]))
    qt_hi[...] = hi
    qt_lo[...] = lo

    f_copies = [pltpu.make_async_remote_copy(
        src_ref=f_out, dst_ref=f_in.at[core], send_sem=f_send.at[c], recv_sem=f_recv.at[core],
        device_id={"tm": above + c}) for c in range(2)]
    b_copies = [pltpu.make_async_remote_copy(
        src_ref=b_out, dst_ref=b_in.at[core], send_sem=b_send.at[c], recv_sem=b_recv.at[core],
        device_id={"tm": below + c}) for c in range(2)]
    f_got = [pltpu.make_async_remote_copy(
        src_ref=f_out, dst_ref=f_in.at[c], send_sem=f_send.at[c], recv_sem=f_recv.at[c],
        device_id={"tm": above + c}) for c in range(2)]
    b_got = [pltpu.make_async_remote_copy(
        src_ref=b_out, dst_ref=b_in.at[c], send_sem=b_send.at[c], recv_sem=b_recv.at[c],
        device_id={"tm": below + c}) for c in range(2)]
    give_f = pltpu.make_async_remote_copy(
        src_ref=side_out, dst_ref=f_side, send_sem=s_send, recv_sem=s_recv,
        device_id={"tm": partner})
    give_b = pltpu.make_async_remote_copy(
        src_ref=side_out, dst_ref=b_side, send_sem=s_send, recv_sem=s_recv,
        device_id={"tm": partner})

    def forward_hop():
        @pl.when(chip == 0)
        def _():
            f_in[0] = init_ref[...]
            f_in[1] = jnp.zeros((1, states), f32)

        @pl.when(chip > 0)
        def _():
            for got in f_got:
                got.wait_recv()

        @pl.when(chip < chips - 1)
        def _():
            v = f_in[0] + f_in[1]
            out = thin(jnp.broadcast_to(v, (8, states)), q_hi[...], q_lo[...])
            f_out[...] = out[0:1] * (1.0 / jnp.sum(v, axis=1, keepdims=True))
            for copy in f_copies:
                copy.start()

        @pl.when(core == 0)
        def _():
            v = f_in[0] + f_in[1]
            out = thin(jnp.broadcast_to(v, (8, states)), h_hi[...], h_lo[...])
            side_out[...] = out[0:1] * (1.0 / jnp.sum(v, axis=1, keepdims=True))
            give_f.start()

    def backward_hop():
        @pl.when(chip == chips - 1)
        def _():
            b_in[0] = jnp.full((1, states), 1.0 / states, f32)
            b_in[1] = jnp.zeros((1, states), f32)

        @pl.when(chip < chips - 1)
        def _():
            for got in b_got:
                got.wait_recv()

        @pl.when(chip > 0)
        def _():
            w = b_in[0] + b_in[1]
            out = thin(jnp.broadcast_to(w, (8, states)), qt_hi[...], qt_lo[...])
            b_out[...] = out[0:1] * (1.0 / jnp.sum(w, axis=1, keepdims=True))
            for copy in b_copies:
                copy.start()

        @pl.when(core == 1)
        def _():
            w = b_in[0] + b_in[1]
            out = thin(jnp.broadcast_to(w, (8, states)), ht_hi[...], ht_lo[...])
            side_out[...] = out[0:1] * (1.0 / jnp.sum(w, axis=1, keepdims=True))
            give_b.start()

    @pl.when(2 * chip < chips)
    def _():
        forward_hop()
        backward_hop()

    @pl.when(2 * chip >= chips)
    def _():
        backward_hop()
        forward_hop()

    @pl.when(core == 0)
    def _():
        f_side[...] = f_in[0] + f_in[1]
        give_b.wait_recv()

    @pl.when(core == 1)
    def _():
        b_side[...] = b_in[0] + b_in[1]
        give_f.wait_recv()

    def unit(x):
        return x * (1.0 / jnp.sum(x, axis=1, keepdims=True))

    fs = [unit(f_side[...])]
    for g in range(SUBS - 1):
        nxt = thin(jnp.broadcast_to(fs[-1], (8, states)), p_hi[g], p_lo[g])
        fs.append(unit(nxt[0:1]))
    bs = [unit(b_side[...])]
    for g in range(SUBS - 1, 0, -1):
        nxt = thin(jnp.broadcast_to(bs[-1], (8, states)), pt_hi[g], pt_lo[g])
        bs.append(unit(nxt[0:1]))
    bs = bs[::-1]
    pad = [jnp.zeros((8 - SUBS, states), f32)]
    f = jnp.concatenate(fs + pad, axis=0)
    b = jnp.concatenate(bs + pad, axis=0)
    b_ref[per - 1] = b
    for i in range(per):
        f = (f * stay + thin(f, w_hi[...], w_lo[...])) * e_ref[i]
        u_ref[i] = f
        j = per - 1 - i
        if j > 0:
            m = b * e_ref[j]
            b = m * stay + thin(m, wt_hi[...], wt_lo[...])
            b_ref[j - 1] = b

    l_ref[...] = jnp.zeros_like(l_ref)
    before = jnp.ones((8, 1), f32)
    for i in range(per):
        u = u_ref[i]
        here = jnp.sum(u, axis=1, keepdims=True)
        logs = jnp.log(here / before)
        before = here
        bb = b_ref[i]
        joint = (u / here) * (bb / jnp.sum(bb, axis=1, keepdims=True))
        occ = states * joint / jnp.sum(joint, axis=1, keepdims=True)
        for g in range(SUBS):
            occ_ref[g * per + i:g * per + i + 1, :] = occ[g:g + 1]
            l_ref[g * per + i:g * per + i + 1, :] = jnp.broadcast_to(logs[g:g + 1], (1, 128))

    ln_ref[...] = jnp.transpose(l_ref[...])[0:1, :steps]

    @pl.when(chip < chips - 1)
    def _():
        for copy in f_copies:
            copy.wait_send()

    @pl.when(chip > 0)
    def _():
        for copy in b_copies:
            copy.wait_send()

    @pl.when(core == 0)
    def _():
        give_cols.wait_send()
        give_f.wait_send()

    @pl.when(core == 1)
    def _():
        give_rows.wait_send()
        give_b.wait_send()


def body(initial_weights, leave_rate, block_weights, block_cols, emission_weights, symbols):
    states = leave_rate.shape[0]
    steps = symbols.shape[0]
    per = steps // SUBS
    vmem = pl.BlockSpec(memory_space=pltpu.VMEM)
    far = pl.BlockSpec(memory_space=pltpu.HBM)
    dma = pltpu.SemaphoreType.DMA
    tall = -(-steps // 128) * 128
    square = (states, states)
    row = pltpu.VMEM((1, states), f32)
    pair = pltpu.VMEM((2, 1, states), f32)
    occupancy, log_norm = pl.pallas_call(
        kernel,
        out_shape=(jax.ShapeDtypeStruct((steps, states), f32),
                   jax.ShapeDtypeStruct((1, steps), f32)),
        in_specs=[vmem, vmem, far, far, far, far],
        out_specs=(vmem, vmem),
        scratch_shapes=[
            pltpu.VMEM(block_weights.shape, f32), pltpu.SMEM(block_cols.shape[::-1], jnp.int32),
            pltpu.VMEM(emission_weights.shape, f32), pltpu.SMEM(symbols.shape, jnp.int32), dma((4,)),
            pltpu.VMEM(square, f32), pltpu.VMEM(square, bf16), pltpu.VMEM(square, bf16),
            pltpu.VMEM((SUBS + 2,) + square, f32),
            pltpu.VMEM((SUBS,) + square, bf16), pltpu.VMEM((SUBS,) + square, bf16),
            pltpu.VMEM(square, bf16), pltpu.VMEM(square, bf16),
            pltpu.VMEM(square, bf16), pltpu.VMEM(square, bf16),
            pltpu.VMEM(square, bf16), pltpu.VMEM(square, bf16),
            pltpu.VMEM((SUBS,) + square, bf16), pltpu.VMEM((SUBS,) + square, bf16),
            pltpu.VMEM(square, bf16), pltpu.VMEM(square, bf16),
            pltpu.VMEM(square, bf16), pltpu.VMEM(square, bf16),
            pltpu.VMEM((per, 8, states), f32), pltpu.VMEM((per, 8, states), f32),
            pltpu.VMEM((per, 8, states), f32), pltpu.VMEM((tall, 128), f32),
            pltpu.VMEM(square, f32), pltpu.VMEM((states, states // 2), f32),
            pltpu.VMEM((states // 2, states), f32),
            pair, row, pair, row, row, row, row,
            dma, dma, dma((2,)), dma((2,)), dma((2,)), dma((2,)), dma, dma,
        ],
        compiler_params=pltpu.CompilerParams(
            collective_id=0, has_side_effects=True, vmem_limit_bytes=64 * 1024 * 1024 - 65536),
    )(initial_weights[None, :], leave_rate[None, :], block_weights, block_cols.T,
      emission_weights, symbols)
    return occupancy, log_norm[0]


def solution(mesh):
    placed = (P(), P(), P(), P(), P(), P(("grp", "tm")))
    return jax.shard_map(
        body,
        mesh=mesh,
        in_specs=placed,
        out_specs=(P(("grp", "tm"), None), P(("grp", "tm"))),
        check_vma=False,
    )
```
